128 devices in a mesh: seq: 16 (over y_hi, x, core), ch: 8 (over z, y_lo).
Axes of the slice: x: 4, y: 4 (y_hi: 2, y_lo: 2; y = y_hi * 2 + y_lo), z: 4, core: 2. Of those that a mesh axis runs over, the one named last changes fastest.
Arguments:
- keys: bfloat16 [4096, 8192], P('seq', 'ch'), may hold values from -6 to 6
- values: bfloat16 [4096, 8192], P('seq', 'ch'), may hold values from -6 to 6
- queries: bfloat16 [4096, 8192], P('seq', 'ch'), may hold values from -6 to 6
- decay: float32 [8192, 16], P('ch'), may hold values from 1 to 600
- residue: float32 [8192, 16], P('ch'), may hold values from -2 to 2
- skip: float32 [8192], P('ch'), may hold values from -4 to 4
- out_weight: bfloat16 [8192, 4096], P('ch', 'seq'), may hold values from -0.0625 to 0.0625
Outputs:
- projected: bfloat16 [4096, 4096], P('seq', 'ch')
The draws below stay inside these ranges and needn't reach their ends.
All inputs are finite; a program needn't handle non-finite values.
Results may differ from the reference program's by a relative error of at most 0.023.
Values may be sent and summed in bfloat16 or wider, within the bound.
No kernel may reach another device: no remote copies, remote signals or barrier semaphores. Data moves between devices by JAX's collectives and lax.ppermute only.
A program may use at most 64 MiB of HBM per device.

```python
import math
import jax
import jax.numpy as jnp
from jax import lax

D = 8192
DOUT = 4096
MODES = 16
SEQ = 4096
N_CH = 8


def steps_of(own_key, dims, pieces, low, largest):
    loudness, own = 1.0, jax.random.fold_in(own_key, 6)
    for position, blocks in pieces:
        heights = jnp.exp(jax.random.uniform(jax.random.fold_in(own, position), (blocks,), jnp.float32, low / len(pieces), largest / len(pieces)))
        loudness = loudness * jnp.repeat(heights, dims[position] // blocks).reshape([-1 if axis == position else 1 for axis in range(len(dims))])
    return loudness


def centred(rng, shape, deviation, reach, cuts=(), dtype=jnp.bfloat16):
    drawn = deviation * jax.random.normal(rng, shape, jnp.float32)
    if cuts:
        drawn = drawn * steps_of(rng, shape, cuts, -0.22, 0.18)
    return jnp.clip(drawn, -reach, reach).astype(dtype)


def setup_inputs(seed: int = 0) -> dict:
    seeds = jax.random.split(jax.random.key(seed), 8)
    keys = centred(seeds[0], (SEQ, D), 1.0, 6.0, ((0, 16), (1, 8)))
    values = centred(seeds[1], (SEQ, D), 1.0, 6.0, ((0, 16), (1, 8)))
    queries = centred(seeds[2], (SEQ, D), 1.0, 6.0, ((0, 16), (1, 8)))
    decay = jnp.clip(jnp.exp(math.log(600.0) - 6.3969297 * jax.random.uniform(seeds[3], (D, MODES), jnp.float32) ** steps_of(seeds[3], (D, MODES), ((0, 8),), -0.2, 0.2)), 1.0, 600.0)
    residue = centred(seeds[4], (D, MODES), 0.35, 2.0, ((0, 8),), jnp.float32)
    skip = centred(seeds[5], (D,), 1.0, 4.0, ((0, 8),), jnp.float32)
    out_weight = centred(seeds[6], (D, DOUT), D ** -0.5, 0.0625, ((0, 8), (1, 16)))
    return {"keys": keys, "values": values, "queries": queries, "decay": decay, "residue": residue, "skip": skip, "out_weight": out_weight}


def convolve_block(operands):
    block_z, block_decay, block_residue, block_skip = operands
    seq_len = block_z.shape[1]
    positions = jnp.arange(seq_len).astype(jnp.float32)
    filt = jnp.zeros(block_z.shape, jnp.float32)
    for mode in range(MODES):
        rate = block_decay[:, mode:mode + 1] / jnp.float32(seq_len)
        filt = filt + block_residue[:, mode:mode + 1] * jnp.sqrt(rate) * jnp.exp(-rate * positions[None, :])
    z_spec = jnp.fft.rfft(block_z, n=2 * seq_len, axis=1)
    f_spec = jnp.fft.rfft(filt, n=2 * seq_len, axis=1)
    conv = jnp.fft.irfft(z_spec * f_spec, n=2 * seq_len, axis=1)[:, :seq_len]
    return conv + block_skip[:, None] * block_z

def reference(keys, values, queries, decay, residue, skip, out_weight):
    seq_len = keys.shape[0]
    width = keys.shape[1]
    mixed = (keys.astype(jnp.float32) * values.astype(jnp.float32)).astype(jnp.bfloat16)
    mixed = lax.optimization_barrier(mixed).astype(jnp.float32)
    block = 256
    groups = width // block
    z_blocks = mixed.T.reshape(groups, block, seq_len)
    filtered = lax.map(convolve_block, (z_blocks, decay.reshape(groups, block, MODES), residue.reshape(groups, block, MODES), skip.reshape(groups, block)))
    filtered = filtered.reshape(width, seq_len).T
    gated = (queries.astype(jnp.float32) * filtered).astype(jnp.bfloat16)
    part_width = width // N_CH
    total = jnp.zeros((seq_len, out_weight.shape[1]), jnp.float32)
    for part in range(N_CH):
        term = jnp.dot(gated[:, part * part_width:(part + 1) * part_width], out_weight[part * part_width:(part + 1) * part_width, :], preferred_element_type=jnp.float32)
        term = lax.optimization_barrier(term.astype(jnp.bfloat16)).astype(jnp.float32)
        total = total + term
    return total.astype(jnp.bfloat16)
```

```python
import jax
import jax.numpy as jnp
from jax import lax
from jax.experimental import pallas as pl
from jax.experimental.pallas import tpu as pltpu
from jax.sharding import Mesh, PartitionSpec as P

SEQ = ("yh", "x", "core")
CH = ("z", "yl")
ALL = SEQ + CH
SIZES = {"yh": 2, "x": 4, "core": 2, "z": 4, "yl": 2}
LANES = 128
ROWS = 8


def shift(value, axis, step):
    size = SIZES[axis]
    return lax.ppermute(value, axis, [(i, (i + step) % size) for i in range(size)])


def spread_rows(keys_ref, values_ref, z_ref):
    steps = keys_ref.shape[0]
    for block in range(ROWS):
        lanes = pl.ds(block * LANES, LANES)
        product = keys_ref[:, lanes].astype(jnp.float32) * values_ref[:, lanes].astype(jnp.float32)
        z_ref[pl.ds(block * steps, steps), :] = product.astype(jnp.bfloat16).astype(jnp.float32)


def end_state_kernel(keys_ref, values_ref, rate_ref, state_ref, z_ref):
    steps = keys_ref.shape[0]
    modes = rate_ref.shape[0]
    spread_rows(keys_ref, values_ref, z_ref)
    keep = [jnp.exp(-rate_ref[n]) for n in range(modes)]

    def step(t, states):
        z = z_ref[pl.ds(t, ROWS, stride=steps), :]
        return tuple(keep[n] * states[n] + z for n in range(modes))

    start = tuple(jnp.zeros((ROWS, LANES), jnp.float32) for _ in range(modes))
    states = lax.fori_loop(0, steps, step, start, unroll=8)
    for n in range(modes):
        state_ref[n] = states[n]


def gated_kernel(
    keys_ref, values_ref, queries_ref, rate_ref, gain_ref, skip_ref, state_ref, out_ref, z_ref, y_ref
):
    steps = keys_ref.shape[0]
    modes = rate_ref.shape[0]
    spread_rows(keys_ref, values_ref, z_ref)
    keep = [jnp.exp(-rate_ref[n]) for n in range(modes)]
    gain = [gain_ref[n] for n in range(modes)]
    skip = skip_ref[...]

    def step(t, states):
        at = pl.ds(t, ROWS, stride=steps)
        z = z_ref[at, :]
        states = tuple(keep[n] * states[n] + z for n in range(modes))
        terms = [gain[n] * states[n] for n in range(modes)] + [skip * z]
        while len(terms) > 1:
            terms = [sum(terms[i : i + 2]) for i in range(0, len(terms), 2)]
        y_ref[at, :] = terms[0]
        return states

    lax.fori_loop(0, steps, step, tuple(state_ref[n] for n in range(modes)), unroll=4)
    for block in range(ROWS):
        lanes = pl.ds(block * LANES, LANES)
        y = y_ref[pl.ds(block * steps, steps), :]
        out_ref[:, lanes] = (queries_ref[:, lanes].astype(jnp.float32) * y).astype(jnp.bfloat16)


def end_state(keys, values, rate):
    steps = keys.shape[0]
    return pl.pallas_call(
        end_state_kernel,
        out_shape=jax.ShapeDtypeStruct(rate.shape, jnp.float32),
        scratch_shapes=[pltpu.VMEM((ROWS * steps, LANES), jnp.float32)],
        compiler_params=pltpu.CompilerParams(vmem_limit_bytes=32 * 1024 * 1024),
        cost_estimate=pl.CostEstimate(flops=9000000, bytes_accessed=1200000, transcendentals=0),
        name="end_state",
    )(keys, values, rate)


def gate(keys, values, queries, rate, gain, skip, state):
    steps = keys.shape[0]
    return pl.pallas_call(
        gated_kernel,
        out_shape=jax.ShapeDtypeStruct(keys.shape, jnp.bfloat16),
        scratch_shapes=[pltpu.VMEM((ROWS * steps, LANES), jnp.float32) for _ in range(2)],
        compiler_params=pltpu.CompilerParams(vmem_limit_bytes=32 * 1024 * 1024),
        cost_estimate=pl.CostEstimate(flops=18000000, bytes_accessed=2500000, transcendentals=0),
        name="gated",
    )(keys, values, queries, rate, gain, skip, state)


def incoming_state(own, rate, steps):
    core, x, yh = (lax.axis_index(name) for name in ("core", "x", "yh"))
    other = shift(own, "core", 1)
    first = jnp.where(core == 0, own, other)
    second = jnp.where(core == 0, other, own)
    hop = rate * jnp.float32(steps)
    pair = jnp.exp(-hop) * first + second
    ring = [pair] + [shift(pair, "x", j) for j in (1, 2, 3)]
    before = jnp.zeros_like(own)
    total = jnp.zeros_like(own)
    for j in range(4):
        source = (x - j) % 4
        total = total + jnp.exp(-hop * (2 * (3 - source)).astype(jnp.float32)) * ring[j]
        if j:
            before = before + jnp.where(x >= j, jnp.exp(-hop * (2.0 * (j - 1))), 0.0) * ring[j]
    earlier = lax.ppermute(total, "yh", [(0, 1)])
    before = before + jnp.where(yh == 1, jnp.exp(-hop * (2 * x).astype(jnp.float32)), 0.0) * earlier
    return jnp.where(core == 0, before, jnp.exp(-hop) * before + first)


def by_mode(array):
    return array.T.reshape(array.shape[1], ROWS, LANES)


def body(keys, values, queries, decay, residue, skip, out_weight):
    steps = keys.shape[0]
    seq_len = steps * 16
    weight = lax.all_gather(out_weight, SEQ, axis=1, tiled=True)
    rate = by_mode(decay) / jnp.float32(seq_len)
    gain = by_mode(residue) * jnp.sqrt(rate)
    own = end_state(keys, values, rate)
    state = incoming_state(own, rate, steps)
    gated = gate(keys, values, queries, rate, gain, skip.reshape(ROWS, LANES), state)
    partial = jnp.dot(gated, weight, preferred_element_type=jnp.float32).astype(jnp.bfloat16)
    blocks = partial.reshape(steps, 8, partial.shape[1] // 8).transpose(1, 0, 2)
    blocks = lax.all_to_all(blocks, CH, 0, 0)
    return blocks.astype(jnp.float32).sum(0).astype(jnp.bfloat16)


def solution(mesh):
    fine = Mesh(
        mesh.devices.reshape(tuple(SIZES[name] for name in ALL)),
        ALL,
    )
    return jax.shard_map(
        body,
        mesh=fine,
        in_specs=(
            P(SEQ, CH),
            P(SEQ, CH),
            P(SEQ, CH),
            P(CH, None),
            P(CH, None),
            P(CH),
            P(CH, SEQ),
        ),
        out_specs=P(SEQ, CH),
        check_vma=False,
    )
```

```python
import functools

import jax
import jax.numpy as jnp
from jax import lax
from jax.experimental import pallas as pl
from jax.experimental.pallas import tpu as pltpu
from jax.sharding import Mesh, PartitionSpec as P

SEQ = ("yh", "x", "core")
CH = ("z", "yl")
ALL = SEQ + CH
SIZES = {"yh": 2, "x": 4, "core": 2, "z": 4, "yl": 2}
LANES = 128
ROWS = 8
CUT = 40


def shift(value, axis, step):
    size = SIZES[axis]
    return lax.ppermute(value, axis, [(i, (i + step) % size) for i in range(size)])


def spread_rows(keys_ref, values_ref, z_ref):
    steps = keys_ref.shape[0]
    for block in range(ROWS):
        lanes = pl.ds(block * LANES, LANES)
        product = keys_ref[:, lanes].astype(jnp.float32) * values_ref[:, lanes].astype(jnp.float32)
        z_ref[pl.ds(block * steps, steps), :] = product.astype(jnp.bfloat16).astype(jnp.float32)


def end_state_kernel(keys_ref, values_ref, rate_ref, state_ref, z_ref):
    steps = keys_ref.shape[0]
    modes = rate_ref.shape[0]
    spread_rows(keys_ref, values_ref, z_ref)
    keep = [jnp.exp(-rate_ref[n]) for n in range(modes)]

    def step(t, states):
        z = z_ref[pl.ds(t, ROWS, stride=steps), :]
        return tuple(keep[n] * states[n] + z for n in range(modes))

    start = tuple(jnp.zeros((ROWS, LANES), jnp.float32) for _ in range(modes))
    states = lax.fori_loop(0, steps, step, start, unroll=8)
    for n in range(modes):
        state_ref[n] = states[n]


def gated_kernel(
    keys_ref, values_ref, queries_ref, rate_ref, gain_ref, skip_ref, state_ref, out_ref, z_ref, y_ref
):
    steps = keys_ref.shape[0]
    modes = rate_ref.shape[0]
    spread_rows(keys_ref, values_ref, z_ref)
    keep = [jnp.exp(-rate_ref[n]) for n in range(modes)]
    gain = [gain_ref[n] for n in range(modes)]
    skip = skip_ref[...]

    def step(t, states):
        at = pl.ds(t, ROWS, stride=steps)
        z = z_ref[at, :]
        states = tuple(keep[n] * states[n] + z for n in range(modes))
        terms = [gain[n] * states[n] for n in range(modes)] + [skip * z]
        while len(terms) > 1:
            terms = [sum(terms[i : i + 2]) for i in range(0, len(terms), 2)]
        y_ref[at, :] = terms[0]
        return states

    lax.fori_loop(0, steps, step, tuple(state_ref[n] for n in range(modes)), unroll=4)
    for block in range(ROWS):
        lanes = pl.ds(block * LANES, LANES)
        y = y_ref[pl.ds(block * steps, steps), :]
        out_ref[:, lanes] = (queries_ref[:, lanes].astype(jnp.float32) * y).astype(jnp.bfloat16)


def end_state(keys, values, rate):
    steps = keys.shape[0]
    return pl.pallas_call(
        end_state_kernel,
        out_shape=jax.ShapeDtypeStruct(rate.shape, jnp.float32),
        scratch_shapes=[pltpu.VMEM((ROWS * steps, LANES), jnp.float32)],
        compiler_params=pltpu.CompilerParams(vmem_limit_bytes=32 * 1024 * 1024),
        cost_estimate=pl.CostEstimate(flops=9000000, bytes_accessed=1200000, transcendentals=0),
        name="end_state",
    )(keys, values, rate)


def gate(keys, values, queries, rate, gain, skip, state):
    steps = keys.shape[0]
    return pl.pallas_call(
        gated_kernel,
        out_shape=jax.ShapeDtypeStruct(keys.shape, jnp.bfloat16),
        scratch_shapes=[pltpu.VMEM((ROWS * steps, LANES), jnp.float32) for _ in range(2)],
        compiler_params=pltpu.CompilerParams(vmem_limit_bytes=32 * 1024 * 1024),
        cost_estimate=pl.CostEstimate(flops=18000000, bytes_accessed=2500000, transcendentals=0),
        name="gated",
    )(keys, values, queries, rate, gain, skip, state)


def incoming_state(own, rate, steps, join, last_join):
    core, x, yh = (lax.axis_index(name) for name in ("core", "x", "yh"))
    other = shift(own, "core", 1)
    first = jnp.where(core == 0, own, other)
    second = jnp.where(core == 0, other, own)
    hop = rate * jnp.float32(steps)
    pair = jnp.exp(-hop) * first + second
    next_pair = shift(pair, "x", 1)
    pair, next_pair = join(pair, next_pair)
    both = shift(jnp.stack([pair, next_pair]), "x", 2)
    ring = [pair, next_pair, both[0], both[1]]
    before = jnp.zeros_like(own)
    total = jnp.zeros_like(own)
    for j in range(4):
        source = (x - j) % 4
        total = total + jnp.exp(-hop * (2 * (3 - source)).astype(jnp.float32)) * ring[j]
        if j:
            before = before + jnp.where(x >= j, jnp.exp(-hop * (2.0 * (j - 1))), 0.0) * ring[j]
    earlier = last_join(lax.ppermute(total, "yh", [(0, 1)]))
    before = before + jnp.where(yh == 1, jnp.exp(-hop * (2 * x).astype(jnp.float32)), 0.0) * earlier
    return jnp.where(core == 0, before, jnp.exp(-hop) * before + first)


def by_mode(array):
    return array.T.reshape(array.shape[1], ROWS, LANES)


def first_weights(own):
    return shift(own, "x", 1), shift(own, "x", 3), shift(own, "yh", 1)


def second_weights(left, right, far):
    cut = far.shape[0] * CUT // 64
    core = lax.axis_index("core")
    opposite = lax.ppermute(
        jnp.where(core == 0, left, right),
        ("x", "core"),
        [(2 * i + c, 2 * ((i + 1 - 2 * c) % 4) + c) for i in range(4) for c in range(2)],
    )
    tops = shift(jnp.stack([left[:cut], right[:cut]]), "yh", 1)
    return opposite, tops, shift(far[cut:], "x", 1), shift(far[cut:], "x", 3)


def third_weights(opposite, far):
    half = far.shape[0] // 2
    return shift(opposite[:half], "yh", 1), shift(far[half:], "x", 2)


def project_kernel(pieces, first_ref, second_ref, slot_ref, *refs):
    near_ref, far_ref = refs[-2:]
    refs = refs[:-2]
    position = 0
    for block, count in enumerate(pieces):
        sums = [None, None]
        row = 0
        for ref in refs[position : position + count]:
            rows = ref.shape[0]
            for half, rows_ref in enumerate((first_ref, second_ref)):
                term = jnp.dot(rows_ref[:, row : row + rows], ref[...], preferred_element_type=jnp.float32)
                sums[half] = term if sums[half] is None else sums[half] + term
            row += rows
        position += count
        turn, side = slot_ref[0, block], slot_ref[1, block]
        near_ref[side, turn] = sums[0].astype(jnp.bfloat16)
        far_ref[turn, side] = sums[1].astype(jnp.bfloat16)


def project(first, second, blocks, slots):
    flat = [piece for block in blocks for piece in block]
    rows, columns = first.shape[0], flat[0].shape[1]
    return pl.pallas_call(
        functools.partial(project_kernel, [len(block) for block in blocks]),
        out_shape=(
            jax.ShapeDtypeStruct((2, 4, rows, columns), jnp.bfloat16),
            jax.ShapeDtypeStruct((4, 2, rows, columns), jnp.bfloat16),
        ),
        in_specs=[pl.BlockSpec(memory_space=pltpu.VMEM)] * 2
        + [pl.BlockSpec(memory_space=pltpu.SMEM)]
        + [pl.BlockSpec(memory_space=pltpu.VMEM)] * len(flat),
        compiler_params=pltpu.CompilerParams(vmem_limit_bytes=40 * 1024 * 1024),
        cost_estimate=pl.CostEstimate(flops=2200000000, bytes_accessed=7000000, transcendentals=0),
        name="project",
    )(first, second, slots, *flat)


def add_up(*terms):
    total = terms[0].astype(jnp.float32)
    for term in terms[1:]:
        total = total + term.astype(jnp.float32)
    return total.astype(jnp.bfloat16)


def body(keys, values, queries, decay, residue, skip, out_weight):
    steps = keys.shape[0]
    seq_len = steps * 16
    core, x, yh, z, yl = (lax.axis_index(name) for name in ("core", "x", "yh", "z", "yl"))
    rounds = [first_weights(out_weight)]
    rate = by_mode(decay) / jnp.float32(seq_len)
    gain = by_mode(residue) * jnp.sqrt(rate)
    own = end_state(keys, values, rate)

    def join(*values):
        values, rounds[0] = lax.optimization_barrier((values, rounds[0]))
        rounds.append(second_weights(*rounds[0]))
        return values

    def last_join(value):
        value, rounds[1] = lax.optimization_barrier((value, rounds[1]))
        rounds.append(third_weights(rounds[1][0], rounds[0][2]))
        return value

    state = incoming_state(own, rate, steps, join, last_join)
    (left, right, far), (opposite, tops, left_end, right_end), far_opposite = rounds
    blocks = [[out_weight], [left], [opposite], [right]]
    blocks += [[far], [tops[0], left_end], list(far_opposite), [tops[1], right_end]]
    gated = gate(keys, values, queries, rate, gain, skip.reshape(ROWS, LANES), state)
    other = shift(gated, "core", 1)
    first = jnp.where(core == 0, gated, other)
    second = jnp.where(core == 0, other, gated)
    column = [(yh ^ side) * 4 + (x - j) % 4 for side in (0, 1) for j in range(4)]
    slots = jnp.stack(
        [
            jnp.stack([(c // 2 - z) % 4 for c in column]),
            jnp.stack([c % 2 ^ yl for c in column]),
        ]
    ).astype(jnp.int32)
    near, far = project(first, second, blocks, slots)
    pair = add_up(near[0], shift(near[1], "yl", 1))
    ring = add_up(far[0], *[shift(far[j], "z", j) for j in (1, 3, 2)])
    top = add_up(pair[0], *[shift(pair[j], "z", j) for j in (1, 3, 2)])
    end = add_up(ring[0], shift(ring[1], "yl", 1))
    mine = jnp.where(core == 0, top, end)
    got = shift(jnp.where(core == 0, end, top), "core", 1)
    return jnp.where(
        core == 0, jnp.concatenate([mine, got], 1), jnp.concatenate([got, mine], 1)
    )


def solution(mesh):
    fine = Mesh(
        mesh.devices.reshape(tuple(SIZES[name] for name in ALL)),
        ALL,
    )
    return jax.shard_map(
        body,
        mesh=fine,
        in_specs=(
            P(SEQ, CH),
            P(SEQ, CH),
            P(SEQ, CH),
            P(CH, None),
            P(CH, None),
            P(CH),
            P(CH, SEQ),
        ),
        out_specs=P(SEQ, CH),
        check_vma=False,
    )
```

```python
import functools

import jax
import jax.numpy as jnp
from jax import lax
from jax.experimental import pallas as pl
from jax.experimental.pallas import tpu as pltpu
from jax.sharding import Mesh, PartitionSpec as P

SEQ = ("yh", "x", "core")
CH = ("z", "yl")
ALL = SEQ + CH
SIZES = {"yh": 2, "x": 4, "core": 2, "z": 4, "yl": 2}
LANES = 128
CUT = 32
ROWS = 8


def shift(value, axis, step):
    size = SIZES[axis]
    return lax.ppermute(value, axis, [(i, (i + step) % size) for i in range(size)])


def spread_rows(keys_ref, values_ref, z_ref):
    steps = keys_ref.shape[0]
    for block in range(ROWS):
        lanes = pl.ds(block * LANES, LANES)
        product = keys_ref[:, lanes].astype(jnp.float32) * values_ref[:, lanes].astype(jnp.float32)
        z_ref[pl.ds(block * steps, steps), :] = product.astype(jnp.bfloat16).astype(jnp.float32)


def spread_modes(array_ref, spread_ref):
    modes = array_ref.shape[0]
    for block in range(ROWS):
        spread_ref[pl.ds(block * modes, modes), :] = array_ref[:, pl.ds(block * LANES, LANES)]
    return [spread_ref[pl.ds(n, ROWS, stride=modes), :] for n in range(modes)]


def end_state_kernel(
    seq_len, keys_ref, values_ref, decay_ref, residue_ref, state_ref, rate_ref, gain_ref, z_ref, spread_ref
):
    steps = keys_ref.shape[0]
    modes = decay_ref.shape[0]
    spread_rows(keys_ref, values_ref, z_ref)
    rate = [decay * jnp.float32(1.0 / seq_len) for decay in spread_modes(decay_ref, spread_ref)]
    keep = [jnp.exp(-r) for r in rate]
    for n in range(modes):
        rate_ref[n] = rate[n]

    def step(t, states):
        z = z_ref[pl.ds(t, ROWS, stride=steps), :]
        return tuple(keep[n] * states[n] + z for n in range(modes))

    start = tuple(jnp.zeros((ROWS, LANES), jnp.float32) for _ in range(modes))
    states = lax.fori_loop(0, steps, step, start, unroll=8)
    for n in range(modes):
        state_ref[n] = states[n]
    residue = spread_modes(residue_ref, spread_ref)
    for n in range(modes):
        gain_ref[n] = residue[n] * jnp.sqrt(rate_ref[n])


def local_kernel(keys_ref, values_ref, rate_ref, gain_ref, skip_ref, y_ref, z_ref):
    steps = keys_ref.shape[0]
    modes = rate_ref.shape[0]
    spread_rows(keys_ref, values_ref, z_ref)
    keep = [jnp.exp(-rate_ref[n]) for n in range(modes)]
    gain = [gain_ref[n] for n in range(modes)]
    skip = skip_ref[...]

    def step(t, states):
        at = pl.ds(t, ROWS, stride=steps)
        z = z_ref[at, :]
        states = tuple(keep[n] * states[n] + z for n in range(modes))
        y_ref[at, :] = tree_sum([gain[n] * states[n] for n in range(modes)] + [skip * z])
        return states

    start = tuple(jnp.zeros((ROWS, LANES), jnp.float32) for _ in range(modes))
    lax.fori_loop(0, steps, step, start, unroll=4)


def gated_kernel(queries_ref, y_ref, rate_ref, gain_ref, state_ref, out_ref, sum_ref):
    steps = queries_ref.shape[0]
    modes = rate_ref.shape[0]
    keep = [jnp.exp(-rate_ref[n]) for n in range(modes)]

    def step(t, terms):
        at = pl.ds(t, ROWS, stride=steps)
        terms = tuple(keep[n] * terms[n] for n in range(modes))
        sum_ref[at, :] = y_ref[at, :] + tree_sum(list(terms))
        return terms

    lax.fori_loop(0, steps, step, tuple(gain_ref[n] * state_ref[n] for n in range(modes)), unroll=8)
    for block in range(ROWS):
        lanes = pl.ds(block * LANES, LANES)
        y = sum_ref[pl.ds(block * steps, steps), :]
        out_ref[:, lanes] = (queries_ref[:, lanes].astype(jnp.float32) * y).astype(jnp.bfloat16)


def tree_sum(terms):
    while len(terms) > 1:
        terms = [sum(terms[i + 1 : i + 2], terms[i]) for i in range(0, len(terms), 2)]
    return terms[0]


def end_state(keys, values, decay, residue, seq_len):
    steps = keys.shape[0]
    modes = decay.shape[1]
    by_mode = jax.ShapeDtypeStruct((modes, ROWS, LANES), jnp.float32)
    return pl.pallas_call(
        functools.partial(end_state_kernel, seq_len),
        out_shape=(by_mode,) * 3,
        scratch_shapes=[
            pltpu.VMEM((ROWS * steps, LANES), jnp.float32),
            pltpu.VMEM((ROWS * modes, LANES), jnp.float32),
        ],
        compiler_params=pltpu.CompilerParams(vmem_limit_bytes=32 * 1024 * 1024),
        cost_estimate=pl.CostEstimate(flops=9000000, bytes_accessed=1200000, transcendentals=0),
        name="end_state",
    )(keys, values, decay.T, residue.T)


def local_part(keys, values, rate, gain, skip):
    steps = keys.shape[0]
    return pl.pallas_call(
        local_kernel,
        out_shape=jax.ShapeDtypeStruct((ROWS * steps, LANES), jnp.float32),
        scratch_shapes=[pltpu.VMEM((ROWS * steps, LANES), jnp.float32)],
        compiler_params=pltpu.CompilerParams(vmem_limit_bytes=32 * 1024 * 1024),
        cost_estimate=pl.CostEstimate(flops=0, bytes_accessed=0, transcendentals=0),
        name="local_part",
    )(keys, values, rate, gain, skip)


def gate(queries, local, rate, gain, state):
    return pl.pallas_call(
        gated_kernel,
        out_shape=jax.ShapeDtypeStruct(queries.shape, jnp.bfloat16),
        scratch_shapes=[pltpu.VMEM(local.shape, jnp.float32)],
        compiler_params=pltpu.CompilerParams(vmem_limit_bytes=32 * 1024 * 1024),
        cost_estimate=pl.CostEstimate(flops=0, bytes_accessed=0, transcendentals=0),
        name="gated",
    )(queries, local, rate, gain, state)


def incoming_state(own, rate, steps, local):
    core, x, yh = (lax.axis_index(name) for name in ("core", "x", "yh"))
    other = shift(own, "core", 1)
    first = jnp.where(core == 0, own, other)
    second = jnp.where(core == 0, other, own)
    hop = rate * jnp.float32(steps)
    pair = jnp.exp(-hop) * first + second
    half = own.shape[0] // 2
    mine = lax.dynamic_slice_in_dim(pair, core * half, half, 0)
    my_hop = lax.dynamic_slice_in_dim(hop, core * half, half, 0)
    pairs = lax.all_to_all(jnp.broadcast_to(mine[None], (8, *mine.shape)), ("yh", "x"), 0, 0)
    pairs, local = lax.optimization_barrier((pairs, local))
    place = yh * 4 + x
    before = jnp.zeros_like(mine)
    for j in range(8):
        weight = jnp.exp(-my_hop * (2 * jnp.maximum(place - 1 - j, 0)).astype(jnp.float32))
        before = before + jnp.where(j < place, weight, 0.0) * pairs[j]
    rest = shift(before, "core", 1)
    before = jnp.where(core == 0, jnp.concatenate([before, rest]), jnp.concatenate([rest, before]))
    return jnp.where(core == 0, before, jnp.exp(-hop) * before + first), local


def both_ways(value, step):
    return lax.ppermute(
        value,
        ("x", "core"),
        [(2 * i + c, 2 * ((i + (1 - 2 * c) * step) % 4) + c) for i in range(4) for c in range(2)],
    )


def first_weights(own):
    return both_ways(own, 1), both_ways(own, -1), shift(own, "yh", 1)


def second_weights(ahead, behind, far):
    cut = far.shape[0] * CUT // 64
    onward = both_ways(jnp.concatenate([ahead, far[:cut]]), 1)
    across = shift(jnp.concatenate([behind, ahead[cut:]]), "yh", 1)
    return shift(far, "x", 2), onward, across


def project_early_kernel(gated_ref, *refs):
    for block, ref in enumerate(refs[:-1]):
        term = jnp.dot(gated_ref[...], ref[...], preferred_element_type=jnp.float32)
        refs[-1][block] = term.astype(jnp.bfloat16)


def project_early(gated, weights):
    return pl.pallas_call(
        project_early_kernel,
        out_shape=jax.ShapeDtypeStruct((len(weights), gated.shape[0], weights[0].shape[1]), jnp.bfloat16),
        compiler_params=pltpu.CompilerParams(vmem_limit_bytes=32 * 1024 * 1024),
        cost_estimate=pl.CostEstimate(flops=0, bytes_accessed=0, transcendentals=0),
        name="project_early",
    )(gated, *weights)


def project_kernel(gated_ref, other_ref, place_ref, early_ref, *refs):
    first_refs, (onward_ref, across_ref, out_ref) = refs[:-3], refs[-3:]
    count = gated_ref.shape[1]
    cut = onward_ref.shape[0] - count
    core = place_ref[2, 0]

    def late(rows_ref):
        yield jnp.dot(rows_ref[...], onward_ref[:count, :], preferred_element_type=jnp.float32)
        yield jnp.dot(rows_ref[...], across_ref[:count, :], preferred_element_type=jnp.float32)
        yield jnp.dot(
            rows_ref[:, :cut], onward_ref[count:, :], preferred_element_type=jnp.float32
        ) + jnp.dot(rows_ref[:, cut:], across_ref[count:, :], preferred_element_type=jnp.float32)

    def put(half, block, term):
        out_ref[half, place_ref[1, block], place_ref[0, block]] = term.astype(jnp.bfloat16)

    for block, ref in enumerate(first_refs):
        put(core, block, early_ref[block])
        put(1 - core, block, jnp.dot(other_ref[...], ref[...], preferred_element_type=jnp.float32))
    for half, rows_ref in ((core, gated_ref), (1 - core, other_ref)):
        for block, term in enumerate(late(rows_ref)):
            put(half, len(first_refs) + block, term)


def project(gated, other, places, early, first, onward, across):
    return pl.pallas_call(
        project_kernel,
        out_shape=jax.ShapeDtypeStruct((2, 2, 4, *early.shape[1:]), jnp.bfloat16),
        in_specs=[pl.BlockSpec(memory_space=pltpu.VMEM)] * 2
        + [pl.BlockSpec(memory_space=pltpu.SMEM)]
        + [pl.BlockSpec(memory_space=pltpu.VMEM)] * (len(first) + 3),
        compiler_params=pltpu.CompilerParams(vmem_limit_bytes=32 * 1024 * 1024),
        cost_estimate=pl.CostEstimate(flops=1500000000, bytes_accessed=7000000, transcendentals=0),
        name="project",
    )(gated, other, places, early, *first, onward, across)


def add_up(*terms):
    total = terms[0].astype(jnp.float32)
    for term in terms[1:]:
        total = total + term.astype(jnp.float32)
    return total.astype(jnp.bfloat16)


def body(keys, values, queries, decay, residue, skip, out_weight):
    steps = keys.shape[0]
    seq_len = steps * 16
    core, x, yh, z, yl = (lax.axis_index(name) for name in ("core", "x", "yh", "z", "yl"))
    first = first_weights(out_weight)
    own, rate, gain = end_state(keys, values, decay, residue, seq_len)
    first, late_gain = lax.optimization_barrier((first, gain))
    local = local_part(keys, values, rate, late_gain, skip.reshape(ROWS, LANES))
    state, local = incoming_state(own, rate, steps, local)
    far_opposite, onward, across = second_weights(*first)
    state, far_opposite = lax.optimization_barrier((state, far_opposite))
    gated = gate(queries, local, rate, gain, state)
    other = shift(gated, "core", 1)
    ahead, behind = 2 * core - 1, 1 - 2 * core
    column = [yh * 4 + (x + j) % 4 for j in (0, ahead, behind)] + [(yh ^ 1) * 4 + x]
    column += [(yh ^ 1) * 4 + (x + 2) % 4, yh * 4 + (x + 2) % 4]
    column += [(yh ^ 1) * 4 + (x + j) % 4 for j in (behind, ahead)]
    places = [[(c // 2 - z) % 4 for c in column], [c % 2 ^ yl for c in column], [core] * 8]
    places = jnp.stack([jnp.stack(row) for row in places]).astype(jnp.int32)
    first = (out_weight, *first, far_opposite)
    near, away = project(gated, other, places, project_early(gated, first), first, onward, across)
    ring = add_up(away[:, 0], *[shift(away[:, j], "z", j) for j in (2, 1, 3)])
    pair = add_up(near[0], shift(near[1], "yl", 1))
    top = add_up(pair[0], *[shift(pair[j], "z", j) for j in (2, 1, 3)])
    end = add_up(ring[0], shift(ring[1], "yl", 1))
    mine = jnp.where(core == 0, top, end)
    got = shift(jnp.where(core == 0, end, top), "core", 1)
    return jnp.where(
        core == 0, jnp.concatenate([mine, got], 1), jnp.concatenate([got, mine], 1)
    )


def solution(mesh):
    fine = Mesh(
        mesh.devices.reshape(tuple(SIZES[name] for name in ALL)),
        ALL,
    )
    return jax.shard_map(
        body,
        mesh=fine,
        in_specs=(
            P(SEQ, CH),
            P(SEQ, CH),
            P(SEQ, CH),
            P(CH, None),
            P(CH, None),
            P(CH),
            P(CH, SEQ),
        ),
        out_specs=P(SEQ, CH),
        check_vma=False,
    )
```

```python
import functools

import jax
import jax.numpy as jnp
from jax import lax
from jax.experimental import pallas as pl
from jax.experimental.pallas import tpu as pltpu
from jax.sharding import Mesh, PartitionSpec as P

SEQ = ("yh", "x", "core")
CH = ("z", "yl")
ALL = SEQ + CH
SIZES = {"yh": 2, "x": 4, "core": 2, "z": 4, "yl": 2}
LANES = 128
CUT = 24
ROWS = 8


def shift(value, axis, step):
    size = SIZES[axis]
    return lax.ppermute(value, axis, [(i, (i + step) % size) for i in range(size)])


def spread_rows(keys_ref, values_ref, z_ref):
    steps = keys_ref.shape[0]
    for block in range(ROWS):
        lanes = pl.ds(block * LANES, LANES)
        product = keys_ref[:, lanes].astype(jnp.float32) * values_ref[:, lanes].astype(jnp.float32)
        z_ref[pl.ds(block * steps, steps), :] = product.astype(jnp.bfloat16).astype(jnp.float32)


def spread_modes(array_ref, spread_ref):
    modes = array_ref.shape[0]
    for block in range(ROWS):
        spread_ref[pl.ds(block * modes, modes), :] = array_ref[:, pl.ds(block * LANES, LANES)]
    return [spread_ref[pl.ds(n, ROWS, stride=modes), :] for n in range(modes)]


def end_state_kernel(
    seq_len, keys_ref, values_ref, decay_ref, state_ref, rate_ref, z_ref, spread_ref
):
    steps = keys_ref.shape[0]
    modes = decay_ref.shape[0]
    spread_rows(keys_ref, values_ref, z_ref)
    rate = [decay * jnp.float32(1.0 / seq_len) for decay in spread_modes(decay_ref, spread_ref)]
    keep = [jnp.exp(-r) for r in rate]
    for n in range(modes):
        rate_ref[n] = rate[n]

    def step(t, states):
        z = z_ref[pl.ds(t, ROWS, stride=steps), :]
        return tuple(keep[n] * states[n] + z for n in range(modes))

    start = tuple(jnp.zeros((ROWS, LANES), jnp.float32) for _ in range(modes))
    states = lax.fori_loop(0, steps, step, start, unroll=8)
    for n in range(modes):
        state_ref[n] = states[n]


def local_kernel(keys_ref, values_ref, rate_ref, residue_ref, skip_ref, y_ref, gain_ref, z_ref, spread_ref):
    steps = keys_ref.shape[0]
    modes = rate_ref.shape[0]
    spread_rows(keys_ref, values_ref, z_ref)
    keep = [jnp.exp(-rate_ref[n]) for n in range(modes)]
    residue = spread_modes(residue_ref, spread_ref)
    gain = [residue[n] * jnp.sqrt(rate_ref[n]) for n in range(modes)]
    for n in range(modes):
        gain_ref[n] = gain[n]
    skip = skip_ref[...]

    def step(t, states):
        at = pl.ds(t, ROWS, stride=steps)
        z = z_ref[at, :]
        states = tuple(keep[n] * states[n] + z for n in range(modes))
        y_ref[at, :] = tree_sum([gain[n] * states[n] for n in range(modes)] + [skip * z])
        return states

    start = tuple(jnp.zeros((ROWS, LANES), jnp.float32) for _ in range(modes))
    lax.fori_loop(0, steps, step, start, unroll=4)


def gated_kernel(queries_ref, y_ref, rate_ref, gain_ref, state_ref, out_ref, sum_ref):
    steps = queries_ref.shape[0]
    modes = rate_ref.shape[0]
    keep = [jnp.exp(-rate_ref[n]) for n in range(modes)]

    def step(t, terms):
        at = pl.ds(t, ROWS, stride=steps)
        terms = tuple(keep[n] * terms[n] for n in range(modes))
        sum_ref[at, :] = y_ref[at, :] + tree_sum(list(terms))
        return terms

    lax.fori_loop(0, steps, step, tuple(gain_ref[n] * state_ref[n] for n in range(modes)), unroll=8)
    for block in range(ROWS):
        lanes = pl.ds(block * LANES, LANES)
        y = sum_ref[pl.ds(block * steps, steps), :]
        out_ref[:, lanes] = (queries_ref[:, lanes].astype(jnp.float32) * y).astype(jnp.bfloat16)


def tree_sum(terms):
    while len(terms) > 1:
        terms = [sum(terms[i + 1 : i + 2], terms[i]) for i in range(0, len(terms), 2)]
    return terms[0]


def end_state(keys, values, decay, seq_len):
    steps = keys.shape[0]
    modes = decay.shape[1]
    by_mode = jax.ShapeDtypeStruct((modes, ROWS, LANES), jnp.float32)
    return pl.pallas_call(
        functools.partial(end_state_kernel, seq_len),
        out_shape=(by_mode,) * 2,
        scratch_shapes=[
            pltpu.VMEM((ROWS * steps, LANES), jnp.float32),
            pltpu.VMEM((ROWS * modes, LANES), jnp.float32),
        ],
        compiler_params=pltpu.CompilerParams(vmem_limit_bytes=32 * 1024 * 1024),
        cost_estimate=pl.CostEstimate(flops=9000000, bytes_accessed=1200000, transcendentals=0),
        name="end_state",
    )(keys, values, decay.T)


def local_part(keys, values, rate, residue, skip):
    steps = keys.shape[0]
    return pl.pallas_call(
        local_kernel,
        out_shape=(
            jax.ShapeDtypeStruct((ROWS * steps, LANES), jnp.float32),
            jax.ShapeDtypeStruct(rate.shape, jnp.float32),
        ),
        scratch_shapes=[
            pltpu.VMEM((ROWS * steps, LANES), jnp.float32),
            pltpu.VMEM((ROWS * rate.shape[0], LANES), jnp.float32),
        ],
        compiler_params=pltpu.CompilerParams(vmem_limit_bytes=32 * 1024 * 1024),
        cost_estimate=pl.CostEstimate(flops=0, bytes_accessed=0, transcendentals=0),
        name="local_part",
    )(keys, values, rate, residue.T, skip)


def gate(queries, local, rate, gain, state):
    return pl.pallas_call(
        gated_kernel,
        out_shape=jax.ShapeDtypeStruct(queries.shape, jnp.bfloat16),
        scratch_shapes=[pltpu.VMEM(local.shape, jnp.float32)],
        compiler_params=pltpu.CompilerParams(vmem_limit_bytes=32 * 1024 * 1024),
        cost_estimate=pl.CostEstimate(flops=0, bytes_accessed=0, transcendentals=0),
        name="gated",
    )(queries, local, rate, gain, state)


def incoming_state(own, rate, steps, local):
    core, x, yh = (lax.axis_index(name) for name in ("core", "x", "yh"))
    other = shift(own, "core", 1)
    first = jnp.where(core == 0, own, other)
    second = jnp.where(core == 0, other, own)
    hop = rate * jnp.float32(steps)
    pair = jnp.exp(-hop) * first + second
    half = own.shape[0] // 2
    mine = lax.dynamic_slice_in_dim(pair, core * half, half, 0)
    my_hop = lax.dynamic_slice_in_dim(hop, core * half, half, 0)
    pairs = lax.all_to_all(jnp.broadcast_to(mine[None], (8, *mine.shape)), ("yh", "x"), 0, 0)
    pairs, local = lax.optimization_barrier((pairs, local))
    place = yh * 4 + x
    before = jnp.zeros_like(mine)
    for j in range(8):
        weight = jnp.exp(-my_hop * (2 * jnp.maximum(place - 1 - j, 0)).astype(jnp.float32))
        before = before + jnp.where(j < place, weight, 0.0) * pairs[j]
    rest = shift(before, "core", 1)
    before = jnp.where(core == 0, jnp.concatenate([before, rest]), jnp.concatenate([rest, before]))
    return jnp.where(core == 0, before, jnp.exp(-hop) * before + first), local


def both_ways(value, step):
    return lax.ppermute(
        value,
        ("x", "core"),
        [(2 * i + c, 2 * ((i + (1 - 2 * c) * step) % 4) + c) for i in range(4) for c in range(2)],
    )


def first_weights(own):
    return both_ways(own, 1), both_ways(own, -1), shift(own, "yh", 1)


def second_weights(ahead, behind, far):
    cut = far.shape[0] * CUT // 64
    onward = both_ways(jnp.concatenate([ahead, far[:cut]]), 1)
    across = shift(jnp.concatenate([behind, ahead[cut:]]), "yh", 1)
    return shift(far, "x", 2), onward, across


def project_early_kernel(gated_ref, *refs):
    for block, ref in enumerate(refs[:-1]):
        term = jnp.dot(gated_ref[...], ref[...], preferred_element_type=jnp.float32)
        refs[-1][block] = term.astype(jnp.bfloat16)


def project_early(gated, weights):
    return pl.pallas_call(
        project_early_kernel,
        out_shape=jax.ShapeDtypeStruct((len(weights), gated.shape[0], weights[0].shape[1]), jnp.bfloat16),
        compiler_params=pltpu.CompilerParams(vmem_limit_bytes=32 * 1024 * 1024),
        cost_estimate=pl.CostEstimate(flops=0, bytes_accessed=0, transcendentals=0),
        name="project_early",
    )(gated, *weights)


def late_blocks(rows_ref, onward_ref, across_ref):
    count = rows_ref.shape[1]
    cut = onward_ref.shape[0] - count
    yield jnp.dot(rows_ref[...], onward_ref[:count, :], preferred_element_type=jnp.float32)
    yield jnp.dot(rows_ref[...], across_ref[:count, :], preferred_element_type=jnp.float32)
    yield jnp.dot(rows_ref[:, :cut], onward_ref[count:, :], preferred_element_type=jnp.float32) + jnp.dot(
        rows_ref[:, cut:], across_ref[count:, :], preferred_element_type=jnp.float32
    )


def project_own_kernel(gated_ref, place_ref, early_ref, onward_ref, across_ref, out_ref):
    early = early_ref.shape[0]
    for block in range(early):
        out_ref[place_ref[0, block], place_ref[1, block]] = early_ref[block]
    for block, term in enumerate(late_blocks(gated_ref, onward_ref, across_ref), early):
        out_ref[place_ref[0, block], place_ref[1, block]] = term.astype(jnp.bfloat16)


def project_other_kernel(other_ref, place_ref, *refs):
    first_refs, (onward_ref, across_ref, out_ref) = refs[:-3], refs[-3:]
    for block, ref in enumerate(first_refs):
        term = jnp.dot(other_ref[...], ref[...], preferred_element_type=jnp.float32)
        out_ref[place_ref[1, block], place_ref[2, block]] = term.astype(jnp.bfloat16)
    for block, term in enumerate(late_blocks(other_ref, onward_ref, across_ref), len(first_refs)):
        out_ref[place_ref[1, block], place_ref[2, block]] = term.astype(jnp.bfloat16)


def project(kernel, lead, rows, places, weights):
    return pl.pallas_call(
        kernel,
        out_shape=jax.ShapeDtypeStruct((*lead, rows.shape[0], weights[-1].shape[1]), jnp.bfloat16),
        in_specs=[pl.BlockSpec(memory_space=pltpu.VMEM), pl.BlockSpec(memory_space=pltpu.SMEM)]
        + [pl.BlockSpec(memory_space=pltpu.VMEM)] * len(weights),
        compiler_params=pltpu.CompilerParams(vmem_limit_bytes=32 * 1024 * 1024),
        cost_estimate=pl.CostEstimate(flops=800000000, bytes_accessed=4000000, transcendentals=0),
        name=kernel.__name__,
    )(rows, places, *weights)


def add_up(*terms):
    total = terms[0].astype(jnp.float32)
    for term in terms[1:]:
        total = total + term.astype(jnp.float32)
    return total.astype(jnp.bfloat16)


def body(keys, values, queries, decay, residue, skip, out_weight):
    steps = keys.shape[0]
    seq_len = steps * 16
    core, x, yh, z, yl = (lax.axis_index(name) for name in ("core", "x", "yh", "z", "yl"))
    first = first_weights(out_weight)
    own, rate = end_state(keys, values, decay, seq_len)
    first, late_rate = lax.optimization_barrier((first, rate))
    local, gain = local_part(keys, values, late_rate, residue, skip.reshape(ROWS, LANES))
    state, local = incoming_state(own, rate, steps, local)
    far_opposite, onward, across = second_weights(*first)
    state, far_opposite = lax.optimization_barrier((state, far_opposite))
    gated = gate(queries, local, rate, gain, state)
    other = shift(gated, "core", 1)
    ahead, behind = 2 * core - 1, 1 - 2 * core
    column = [yh * 4 + (x + j) % 4 for j in (0, ahead, behind)] + [(yh ^ 1) * 4 + x]
    column += [(yh ^ 1) * 4 + (x + 2) % 4, yh * 4 + (x + 2) % 4]
    column += [(yh ^ 1) * 4 + (x + j) % 4 for j in (behind, ahead)]
    places = [[(c // 2 - z) % 4 for c in column], [c % 2 ^ yl for c in column], [c // 2 for c in column]]
    places = jnp.stack([jnp.stack(row) for row in places]).astype(jnp.int32)
    first = (out_weight, *first, far_opposite)
    other, early = lax.optimization_barrier((other, project_early(gated, first)))
    near = project(project_other_kernel, (2, 4), other, places, (*first, onward, across))
    near, gated = lax.optimization_barrier((near, gated))
    away = project(project_own_kernel, (4, 2), gated, places, (early, onward, across))
    pair = add_up(near[0], shift(near[1], "yl", 1))
    got = shift(add_up(*lax.all_to_all(pair, "z", 0, 0)), "core", 1)
    ring = add_up(away[0], *[shift(away[j], "z", j) for j in (2, 1, 3)])
    kept = add_up(ring[0], shift(ring[1], "yl", 1))
    return jnp.where(
        core == 0, jnp.concatenate([kept, got], 1), jnp.concatenate([got, kept], 1)
    )


def solution(mesh):
    fine = Mesh(
        mesh.devices.reshape(tuple(SIZES[name] for name in ALL)),
        ALL,
    )
    return jax.shard_map(
        body,
        mesh=fine,
        in_specs=(
            P(SEQ, CH),
            P(SEQ, CH),
            P(SEQ, CH),
            P(CH, None),
            P(CH, None),
            P(CH),
            P(CH, SEQ),
        ),
        out_specs=P(SEQ, CH),
        check_vma=False,
    )
```

```python
import functools

import jax
import jax.numpy as jnp
from jax import lax
from jax.experimental import pallas as pl
from jax.experimental.pallas import tpu as pltpu
from jax.sharding import Mesh, PartitionSpec as P

SEQ = ("yh", "x", "core")
CH = ("z", "yl")
ALL = SEQ + CH
SIZES = {"yh": 2, "x": 4, "core": 2, "z": 4, "yl": 2}
LANES = 128
CUT = 26
ROWS = 8


def shift(value, axis, step):
    size = SIZES[axis]
    return lax.ppermute(value, axis, [(i, (i + step) % size) for i in range(size)])


def spread_rows(keys_ref, values_ref, z_ref):
    steps = keys_ref.shape[0]
    for block in range(ROWS):
        lanes = pl.ds(block * LANES, LANES)
        product = keys_ref[:, lanes].astype(jnp.float32) * values_ref[:, lanes].astype(jnp.float32)
        z_ref[pl.ds(block * steps, steps), :] = product.astype(jnp.bfloat16).astype(jnp.float32)


def spread_modes(array_ref, spread_ref):
    modes = array_ref.shape[0]
    for block in range(ROWS):
        spread_ref[pl.ds(block * modes, modes), :] = array_ref[:, pl.ds(block * LANES, LANES)]
    return [spread_ref[pl.ds(n, ROWS, stride=modes), :] for n in range(modes)]


def end_state_kernel(
    seq_len, keys_ref, values_ref, decay_ref, state_ref, rate_ref, z_ref, spread_ref
):
    steps = keys_ref.shape[0]
    modes = decay_ref.shape[0]
    spread_rows(keys_ref, values_ref, z_ref)
    rate = [decay * jnp.float32(1.0 / seq_len) for decay in spread_modes(decay_ref, spread_ref)]
    keep = [jnp.exp(-r) for r in rate]
    for n in range(modes):
        rate_ref[n] = rate[n]

    def step(t, states):
        z = z_ref[pl.ds(t, ROWS, stride=steps), :]
        return tuple(keep[n] * states[n] + z for n in range(modes))

    start = tuple(jnp.zeros((ROWS, LANES), jnp.float32) for _ in range(modes))
    states = lax.fori_loop(0, steps, step, start, unroll=8)
    for n in range(modes):
        state_ref[n] = states[n]


def local_kernel(keys_ref, values_ref, rate_ref, residue_ref, skip_ref, y_ref, gain_ref, z_ref, spread_ref):
    steps = keys_ref.shape[0]
    modes = rate_ref.shape[0]
    spread_rows(keys_ref, values_ref, z_ref)
    keep = [jnp.exp(-rate_ref[n]) for n in range(modes)]
    residue = spread_modes(residue_ref, spread_ref)
    gain = [residue[n] * jnp.sqrt(rate_ref[n]) for n in range(modes)]
    for n in range(modes):
        gain_ref[n] = gain[n]
    skip = skip_ref[...]

    def step(t, states):
        at = pl.ds(t, ROWS, stride=steps)
        z = z_ref[at, :]
        states = tuple(keep[n] * states[n] + z for n in range(modes))
        y_ref[at, :] = tree_sum([gain[n] * states[n] for n in range(modes)] + [skip * z])
        return states

    start = tuple(jnp.zeros((ROWS, LANES), jnp.float32) for _ in range(modes))
    lax.fori_loop(0, steps, step, start, unroll=4)


def gated_kernel(queries_ref, y_ref, rate_ref, gain_ref, state_ref, out_ref, sum_ref):
    steps = queries_ref.shape[0]
    modes = rate_ref.shape[0]
    keep = [jnp.exp(-rate_ref[n]) for n in range(modes)]

    def step(t, terms):
        at = pl.ds(t, ROWS, stride=steps)
        terms = tuple(keep[n] * terms[n] for n in range(modes))
        sum_ref[at, :] = y_ref[at, :] + tree_sum(list(terms))
        return terms

    lax.fori_loop(0, steps, step, tuple(gain_ref[n] * state_ref[n] for n in range(modes)), unroll=8)
    for block in range(ROWS):
        lanes = pl.ds(block * LANES, LANES)
        y = sum_ref[pl.ds(block * steps, steps), :]
        out_ref[:, lanes] = (queries_ref[:, lanes].astype(jnp.float32) * y).astype(jnp.bfloat16)


def tree_sum(terms):
    while len(terms) > 1:
        terms = [sum(terms[i + 1 : i + 2], terms[i]) for i in range(0, len(terms), 2)]
    return terms[0]


def end_state(keys, values, decay, seq_len):
    steps = keys.shape[0]
    modes = decay.shape[1]
    by_mode = jax.ShapeDtypeStruct((modes, ROWS, LANES), jnp.float32)
    return pl.pallas_call(
        functools.partial(end_state_kernel, seq_len),
        out_shape=(by_mode,) * 2,
        scratch_shapes=[
            pltpu.VMEM((ROWS * steps, LANES), jnp.float32),
            pltpu.VMEM((ROWS * modes, LANES), jnp.float32),
        ],
        compiler_params=pltpu.CompilerParams(vmem_limit_bytes=32 * 1024 * 1024),
        cost_estimate=pl.CostEstimate(flops=9000000, bytes_accessed=1200000, transcendentals=0),
        name="end_state",
    )(keys, values, decay.T)


def local_part(keys, values, rate, residue, skip):
    steps = keys.shape[0]
    return pl.pallas_call(
        local_kernel,
        out_shape=(
            jax.ShapeDtypeStruct((ROWS * steps, LANES), jnp.float32),
            jax.ShapeDtypeStruct(rate.shape, jnp.float32),
        ),
        scratch_shapes=[
            pltpu.VMEM((ROWS * steps, LANES), jnp.float32),
            pltpu.VMEM((ROWS * rate.shape[0], LANES), jnp.float32),
        ],
        compiler_params=pltpu.CompilerParams(vmem_limit_bytes=32 * 1024 * 1024),
        cost_estimate=pl.CostEstimate(flops=0, bytes_accessed=0, transcendentals=0),
        name="local_part",
    )(keys, values, rate, residue.T, skip)


def gate(queries, local, rate, gain, state):
    return pl.pallas_call(
        gated_kernel,
        out_shape=jax.ShapeDtypeStruct(queries.shape, jnp.bfloat16),
        scratch_shapes=[pltpu.VMEM(local.shape, jnp.float32)],
        compiler_params=pltpu.CompilerParams(vmem_limit_bytes=32 * 1024 * 1024),
        cost_estimate=pl.CostEstimate(flops=0, bytes_accessed=0, transcendentals=0),
        name="gated",
    )(queries, local, rate, gain, state)


def incoming_state(own, rate, steps, local):
    core, x, yh = (lax.axis_index(name) for name in ("core", "x", "yh"))
    other = shift(own, "core", 1)
    first = jnp.where(core == 0, own, other)
    second = jnp.where(core == 0, other, own)
    hop = rate * jnp.float32(steps)
    pair = jnp.exp(-hop) * first + second
    half = own.shape[0] // 2
    mine = lax.dynamic_slice_in_dim(pair, core * half, half, 0)
    my_hop = lax.dynamic_slice_in_dim(hop, core * half, half, 0)
    pairs = lax.all_to_all(jnp.broadcast_to(mine[None], (8, *mine.shape)), ("yh", "x"), 0, 0)
    pairs, local = lax.optimization_barrier((pairs, local))
    place = yh * 4 + x
    before = jnp.zeros_like(mine)
    for j in range(8):
        weight = jnp.exp(-my_hop * (2 * jnp.maximum(place - 1 - j, 0)).astype(jnp.float32))
        before = before + jnp.where(j < place, weight, 0.0) * pairs[j]
    rest = shift(before, "core", 1)
    before = jnp.where(core == 0, jnp.concatenate([before, rest]), jnp.concatenate([rest, before]))
    return jnp.where(core == 0, before, jnp.exp(-hop) * before + first), local


def both_ways(value, step):
    return lax.ppermute(
        value,
        ("x", "core"),
        [(2 * i + c, 2 * ((i + (1 - 2 * c) * step) % 4) + c) for i in range(4) for c in range(2)],
    )


def first_weights(own):
    return both_ways(own, 1), both_ways(own, -1), shift(own, "yh", 1)


def second_weights(ahead, behind, far):
    cut = far.shape[0] * CUT // 64
    onward = both_ways(jnp.concatenate([ahead, far[:cut]]), 1)
    across = shift(jnp.concatenate([behind, ahead[cut:]]), "yh", 1)
    return shift(far, "x", 2), onward, across


def project_early_kernel(gated_ref, *refs):
    for block, ref in enumerate(refs[:-1]):
        term = jnp.dot(gated_ref[...], ref[...], preferred_element_type=jnp.float32)
        refs[-1][block] = term.astype(jnp.bfloat16)


def project_early(gated, weights):
    return pl.pallas_call(
        project_early_kernel,
        out_shape=jax.ShapeDtypeStruct((len(weights), gated.shape[0], weights[0].shape[1]), jnp.bfloat16),
        compiler_params=pltpu.CompilerParams(vmem_limit_bytes=32 * 1024 * 1024),
        cost_estimate=pl.CostEstimate(flops=0, bytes_accessed=0, transcendentals=0),
        name="project_early",
    )(gated, *weights)


def late_blocks(rows_ref, onward_ref, across_ref):
    count = rows_ref.shape[1]
    cut = onward_ref.shape[0] - count
    yield jnp.dot(rows_ref[...], onward_ref[:count, :], preferred_element_type=jnp.float32)
    yield jnp.dot(rows_ref[...], across_ref[:count, :], preferred_element_type=jnp.float32)
    yield jnp.dot(rows_ref[:, :cut], onward_ref[count:, :], preferred_element_type=jnp.float32) + jnp.dot(
        rows_ref[:, cut:], across_ref[count:, :], preferred_element_type=jnp.float32
    )


def project_own_kernel(gated_ref, place_ref, early_ref, onward_ref, across_ref, out_ref):
    early = early_ref.shape[0]
    for block in range(early):
        out_ref[place_ref[0, block], place_ref[1, block]] = early_ref[block]
    for block, term in enumerate(late_blocks(gated_ref, onward_ref, across_ref), early):
        out_ref[place_ref[0, block], place_ref[1, block]] = term.astype(jnp.bfloat16)


def project_other_kernel(other_ref, place_ref, *refs):
    first_refs, (onward_ref, across_ref, out_ref) = refs[:-3], refs[-3:]
    for block, ref in enumerate(first_refs):
        term = jnp.dot(other_ref[...], ref[...], preferred_element_type=jnp.float32)
        out_ref[place_ref[1, block], place_ref[2, block]] = term.astype(jnp.bfloat16)
    for block, term in enumerate(late_blocks(other_ref, onward_ref, across_ref), len(first_refs)):
        out_ref[place_ref[1, block], place_ref[2, block]] = term.astype(jnp.bfloat16)


def project(kernel, lead, rows, places, weights):
    return pl.pallas_call(
        kernel,
        out_shape=jax.ShapeDtypeStruct((*lead, rows.shape[0], weights[-1].shape[1]), jnp.bfloat16),
        in_specs=[pl.BlockSpec(memory_space=pltpu.VMEM), pl.BlockSpec(memory_space=pltpu.SMEM)]
        + [pl.BlockSpec(memory_space=pltpu.VMEM)] * len(weights),
        compiler_params=pltpu.CompilerParams(vmem_limit_bytes=32 * 1024 * 1024),
        cost_estimate=pl.CostEstimate(flops=800000000, bytes_accessed=4000000, transcendentals=0),
        name=kernel.__name__,
    )(rows, places, *weights)


def add_up(*terms):
    total = terms[0].astype(jnp.float32)
    for term in terms[1:]:
        total = total + term.astype(jnp.float32)
    return total.astype(jnp.bfloat16)


def add_kernel(left_ref, right_ref, out_ref):
    out_ref[...] = (left_ref[...].astype(jnp.float32) + right_ref[...].astype(jnp.float32)).astype(jnp.bfloat16)


def add_pair(left, right):
    return pl.pallas_call(
        add_kernel,
        out_shape=jax.ShapeDtypeStruct(left.shape, left.dtype),
        compiler_params=pltpu.CompilerParams(vmem_limit_bytes=32 * 1024 * 1024),
        cost_estimate=pl.CostEstimate(flops=0, bytes_accessed=1500000, transcendentals=0),
        name="add_pair",
    )(left, right)


def body(keys, values, queries, decay, residue, skip, out_weight):
    steps = keys.shape[0]
    seq_len = steps * 16
    core, x, yh, z, yl = (lax.axis_index(name) for name in ("core", "x", "yh", "z", "yl"))
    first = first_weights(out_weight)
    own, rate = end_state(keys, values, decay, seq_len)
    first, late_rate = lax.optimization_barrier((first, rate))
    local, gain = local_part(keys, values, late_rate, residue, skip.reshape(ROWS, LANES))
    state, local = incoming_state(own, rate, steps, local)
    far_opposite, onward, across = second_weights(*first)
    state, far_opposite = lax.optimization_barrier((state, far_opposite))
    gated = gate(queries, local, rate, gain, state)
    other = shift(gated, "core", 1)
    ahead, behind = 2 * core - 1, 1 - 2 * core
    column = [yh * 4 + (x + j) % 4 for j in (0, ahead, behind)] + [(yh ^ 1) * 4 + x]
    column += [(yh ^ 1) * 4 + (x + 2) % 4, yh * 4 + (x + 2) % 4]
    column += [(yh ^ 1) * 4 + (x + j) % 4 for j in (behind, ahead)]
    places = [[(c // 2 - z) % 4 for c in column], [c % 2 ^ yl for c in column], [c // 2 for c in column]]
    places = jnp.stack([jnp.stack(row) for row in places]).astype(jnp.int32)
    first = (out_weight, *first, far_opposite)
    other, early = lax.optimization_barrier((other, project_early(gated, first)))
    near = project(project_other_kernel, (2, 4), other, places, (*first, onward, across))
    near, gated = lax.optimization_barrier((near, gated))
    away = project(project_own_kernel, (4, 2), gated, places, (early, onward, across))
    pair = add_pair(near[0], shift(near[1], "yl", 1))
    got = shift(add_up(*lax.all_to_all(pair, "z", 0, 0)), "core", 1)
    ring = add_up(away[0], *[shift(away[j], "z", j) for j in (2, 1, 3)])
    kept = add_up(ring[0], shift(ring[1], "yl", 1))
    return jnp.where(
        core == 0, jnp.concatenate([kept, got], 1), jnp.concatenate([got, kept], 1)
    )


def solution(mesh):
    fine = Mesh(
        mesh.devices.reshape(tuple(SIZES[name] for name in ALL)),
        ALL,
    )
    return jax.shard_map(
        body,
        mesh=fine,
        in_specs=(
            P(SEQ, CH),
            P(SEQ, CH),
            P(SEQ, CH),
            P(CH, None),
            P(CH, None),
            P(CH),
            P(CH, SEQ),
        ),
        out_specs=P(SEQ, CH),
        check_vma=False,
    )
```

```python
import functools

import jax
import jax.numpy as jnp
from jax import lax
from jax.experimental import pallas as pl
from jax.experimental.pallas import tpu as pltpu
from jax.sharding import Mesh, PartitionSpec as P

SEQ = ("yh", "x", "core")
CH = ("z", "yl")
ALL = SEQ + CH
SIZES = {"yh": 2, "x": 4, "core": 2, "z": 4, "yl": 2}
LANES = 128
CUT = 26
ROWS = 8


def shift(value, axis, step):
    size = SIZES[axis]
    return lax.ppermute(value, axis, [(i, (i + step) % size) for i in range(size)])


def spread_rows(keys_ref, values_ref, z_ref):
    steps = keys_ref.shape[0]
    for block in range(ROWS):
        lanes = pl.ds(block * LANES, LANES)
        product = keys_ref[:, lanes].astype(jnp.float32) * values_ref[:, lanes].astype(jnp.float32)
        z_ref[pl.ds(block * steps, steps), :] = product.astype(jnp.bfloat16).astype(jnp.float32)


def spread_modes(array_ref, spread_ref):
    modes = array_ref.shape[0]
    for block in range(ROWS):
        spread_ref[pl.ds(block * modes, modes), :] = array_ref[:, pl.ds(block * LANES, LANES)]
    return [spread_ref[pl.ds(n, ROWS, stride=modes), :] for n in range(modes)]


def end_state_kernel(
    seq_len, keys_ref, values_ref, decay_ref, state_ref, rate_ref, z_ref, spread_ref
):
    steps = keys_ref.shape[0]
    modes = decay_ref.shape[0]
    spread_rows(keys_ref, values_ref, z_ref)
    rate = [decay * jnp.float32(1.0 / seq_len) for decay in spread_modes(decay_ref, spread_ref)]
    keep = [jnp.exp(-r) for r in rate]
    for n in range(modes):
        rate_ref[n] = rate[n]

    def step(t, states):
        z = z_ref[pl.ds(t, ROWS, stride=steps), :]
        return tuple(keep[n] * states[n] + z for n in range(modes))

    start = tuple(jnp.zeros((ROWS, LANES), jnp.float32) for _ in range(modes))
    states = lax.fori_loop(0, steps, step, start, unroll=8)
    for n in range(modes):
        state_ref[n] = states[n]


def local_kernel(keys_ref, values_ref, rate_ref, residue_ref, skip_ref, y_ref, gain_ref, z_ref, spread_ref):
    steps = keys_ref.shape[0]
    modes = rate_ref.shape[0]
    spread_rows(keys_ref, values_ref, z_ref)
    keep = [jnp.exp(-rate_ref[n]) for n in range(modes)]
    residue = spread_modes(residue_ref, spread_ref)
    gain = [residue[n] * jnp.sqrt(rate_ref[n]) for n in range(modes)]
    for n in range(modes):
        gain_ref[n] = gain[n]
    skip = skip_ref[...]

    def step(t, states):
        at = pl.ds(t, ROWS, stride=steps)
        z = z_ref[at, :]
        states = tuple(keep[n] * states[n] + z for n in range(modes))
        y_ref[at, :] = tree_sum([gain[n] * states[n] for n in range(modes)] + [skip * z])
        return states

    start = tuple(jnp.zeros((ROWS, LANES), jnp.float32) for _ in range(modes))
    lax.fori_loop(0, steps, step, start, unroll=4)


def gated_kernel(queries_ref, y_ref, rate_ref, gain_ref, state_ref, out_ref, sum_ref):
    steps = queries_ref.shape[0]
    modes = rate_ref.shape[0]
    keep = [jnp.exp(-rate_ref[n]) for n in range(modes)]

    def step(t, terms):
        at = pl.ds(t, ROWS, stride=steps)
        terms = tuple(keep[n] * terms[n] for n in range(modes))
        sum_ref[at, :] = y_ref[at, :] + tree_sum(list(terms))
        return terms

    lax.fori_loop(0, steps, step, tuple(gain_ref[n] * state_ref[n] for n in range(modes)), unroll=8)
    for block in range(ROWS):
        lanes = pl.ds(block * LANES, LANES)
        y = sum_ref[pl.ds(block * steps, steps), :]
        out_ref[:, lanes] = (queries_ref[:, lanes].astype(jnp.float32) * y).astype(jnp.bfloat16)


def tree_sum(terms):
    while len(terms) > 1:
        terms = [sum(terms[i + 1 : i + 2], terms[i]) for i in range(0, len(terms), 2)]
    return terms[0]


def end_state(keys, values, decay, seq_len):
    steps = keys.shape[0]
    modes = decay.shape[1]
    by_mode = jax.ShapeDtypeStruct((modes, ROWS, LANES), jnp.float32)
    return pl.pallas_call(
        functools.partial(end_state_kernel, seq_len),
        out_shape=(by_mode,) * 2,
        scratch_shapes=[
            pltpu.VMEM((ROWS * steps, LANES), jnp.float32),
            pltpu.VMEM((ROWS * modes, LANES), jnp.float32),
        ],
        compiler_params=pltpu.CompilerParams(vmem_limit_bytes=32 * 1024 * 1024),
        cost_estimate=pl.CostEstimate(flops=9000000, bytes_accessed=1200000, transcendentals=0),
        name="end_state",
    )(keys, values, decay.T)


def local_part(keys, values, rate, residue, skip):
    steps = keys.shape[0]
    return pl.pallas_call(
        local_kernel,
        out_shape=(
            jax.ShapeDtypeStruct((ROWS * steps, LANES), jnp.float32),
            jax.ShapeDtypeStruct(rate.shape, jnp.float32),
        ),
        scratch_shapes=[
            pltpu.VMEM((ROWS * steps, LANES), jnp.float32),
            pltpu.VMEM((ROWS * rate.shape[0], LANES), jnp.float32),
        ],
        compiler_params=pltpu.CompilerParams(vmem_limit_bytes=32 * 1024 * 1024),
        cost_estimate=pl.CostEstimate(flops=0, bytes_accessed=0, transcendentals=0),
        name="local_part",
    )(keys, values, rate, residue.T, skip)


def gate(queries, local, rate, gain, state):
    return pl.pallas_call(
        gated_kernel,
        out_shape=jax.ShapeDtypeStruct(queries.shape, jnp.bfloat16),
        scratch_shapes=[pltpu.VMEM(local.shape, jnp.float32)],
        compiler_params=pltpu.CompilerParams(vmem_limit_bytes=32 * 1024 * 1024),
        cost_estimate=pl.CostEstimate(flops=0, bytes_accessed=0, transcendentals=0),
        name="gated",
    )(queries, local, rate, gain, state)


def incoming_state(own, rate, steps, local):
    core, x, yh = (lax.axis_index(name) for name in ("core", "x", "yh"))
    other = shift(own, "core", 1)
    first = jnp.where(core == 0, own, other)
    second = jnp.where(core == 0, other, own)
    hop = rate * jnp.float32(steps)
    pair = jnp.exp(-hop) * first + second
    half = own.shape[0] // 2
    mine = lax.dynamic_slice_in_dim(pair, core * half, half, 0)
    my_hop = lax.dynamic_slice_in_dim(hop, core * half, half, 0)
    pairs = lax.all_to_all(jnp.broadcast_to(mine[None], (8, *mine.shape)), ("yh", "x"), 0, 0)
    pairs, local = lax.optimization_barrier((pairs, local))
    place = yh * 4 + x
    before = jnp.zeros_like(mine)
    for j in range(8):
        weight = jnp.exp(-my_hop * (2 * jnp.maximum(place - 1 - j, 0)).astype(jnp.float32))
        before = before + jnp.where(j < place, weight, 0.0) * pairs[j]
    rest = shift(before, "core", 1)
    before = jnp.where(core == 0, jnp.concatenate([before, rest]), jnp.concatenate([rest, before]))
    return jnp.where(core == 0, before, jnp.exp(-hop) * before + first), local


def both_ways(value, step):
    return lax.ppermute(
        value,
        ("x", "core"),
        [(2 * i + c, 2 * ((i + (1 - 2 * c) * step) % 4) + c) for i in range(4) for c in range(2)],
    )


def first_weights(own):
    return both_ways(own, 1), both_ways(own, -1), shift(own, "yh", 1)


def second_weights(ahead, behind, far):
    cut = far.shape[0] * CUT // 64
    onward = both_ways(jnp.concatenate([ahead, far[:cut]]), 1)
    across = shift(jnp.concatenate([behind, ahead[cut:]]), "yh", 1)
    return shift(far, "x", 2), onward, across


def project_early_kernel(gated_ref, *refs):
    for block, ref in enumerate(refs[:-1]):
        term = jnp.dot(gated_ref[...], ref[...], preferred_element_type=jnp.float32)
        refs[-1][block] = term.astype(jnp.bfloat16)


def project_early(gated, weights):
    return pl.pallas_call(
        project_early_kernel,
        out_shape=jax.ShapeDtypeStruct((len(weights), gated.shape[0], weights[0].shape[1]), jnp.bfloat16),
        compiler_params=pltpu.CompilerParams(vmem_limit_bytes=32 * 1024 * 1024),
        cost_estimate=pl.CostEstimate(flops=0, bytes_accessed=0, transcendentals=0),
        name="project_early",
    )(gated, *weights)


def late_blocks(rows_ref, onward_ref, across_ref):
    count = rows_ref.shape[1]
    cut = onward_ref.shape[0] - count
    yield jnp.dot(rows_ref[...], onward_ref[:count, :], preferred_element_type=jnp.float32)
    yield jnp.dot(rows_ref[...], across_ref[:count, :], preferred_element_type=jnp.float32)
    yield jnp.dot(rows_ref[:, :cut], onward_ref[count:, :], preferred_element_type=jnp.float32) + jnp.dot(
        rows_ref[:, cut:], across_ref[count:, :], preferred_element_type=jnp.float32
    )


def project_own_kernel(gated_ref, place_ref, early_ref, onward_ref, across_ref, out_ref):
    early = early_ref.shape[0]
    for block in range(early):
        out_ref[place_ref[0, block], place_ref[1, block]] = early_ref[block]
    for block, term in enumerate(late_blocks(gated_ref, onward_ref, across_ref), early):
        out_ref[place_ref[0, block], place_ref[1, block]] = term.astype(jnp.bfloat16)


def project_other_kernel(other_ref, place_ref, *refs):
    first_refs, (onward_ref, across_ref, out_ref) = refs[:-3], refs[-3:]
    for block, ref in enumerate(first_refs):
        term = jnp.dot(other_ref[...], ref[...], preferred_element_type=jnp.float32)
        out_ref[place_ref[1, block], place_ref[2, block]] = term.astype(jnp.bfloat16)
    for block, term in enumerate(late_blocks(other_ref, onward_ref, across_ref), len(first_refs)):
        out_ref[place_ref[1, block], place_ref[2, block]] = term.astype(jnp.bfloat16)


def project(kernel, lead, rows, places, weights):
    return pl.pallas_call(
        kernel,
        out_shape=jax.ShapeDtypeStruct((*lead, rows.shape[0], weights[-1].shape[1]), jnp.bfloat16),
        in_specs=[pl.BlockSpec(memory_space=pltpu.VMEM), pl.BlockSpec(memory_space=pltpu.SMEM)]
        + [pl.BlockSpec(memory_space=pltpu.VMEM)] * len(weights),
        compiler_params=pltpu.CompilerParams(vmem_limit_bytes=32 * 1024 * 1024),
        cost_estimate=pl.CostEstimate(flops=800000000, bytes_accessed=4000000, transcendentals=0),
        name=kernel.__name__,
    )(rows, places, *weights)


def add_up(*terms):
    total = terms[0].astype(jnp.float32)
    for term in terms[1:]:
        total = total + term.astype(jnp.float32)
    return total.astype(jnp.bfloat16)


def add_kernel(left_ref, right_ref, out_ref):
    out_ref[...] = (left_ref[...].astype(jnp.float32) + right_ref[...].astype(jnp.float32)).astype(jnp.bfloat16)


def add_pair(left, right):
    return pl.pallas_call(
        add_kernel,
        out_shape=jax.ShapeDtypeStruct(left.shape, left.dtype),
        compiler_params=pltpu.CompilerParams(vmem_limit_bytes=32 * 1024 * 1024),
        cost_estimate=pl.CostEstimate(flops=0, bytes_accessed=1500000, transcendentals=0),
        name="add_pair",
    )(left, right)


def body(keys, values, queries, decay, residue, skip, out_weight):
    steps = keys.shape[0]
    seq_len = steps * 16
    core, x, yh, z, yl = (lax.axis_index(name) for name in ("core", "x", "yh", "z", "yl"))
    first = first_weights(out_weight)
    own, rate = end_state(keys, values, decay, seq_len)
    first, late_rate = lax.optimization_barrier((first, rate))
    local, gain = local_part(keys, values, late_rate, residue, skip.reshape(ROWS, LANES))
    state, local = incoming_state(own, rate, steps, local)
    far_opposite, onward, across = second_weights(*first)
    state, far_opposite = lax.optimization_barrier((state, far_opposite))
    gated = gate(queries, local, rate, gain, state)
    other = shift(gated, "core", 1)
    ahead, behind = 2 * core - 1, 1 - 2 * core
    column = [yh * 4 + (x + j) % 4 for j in (0, ahead, behind)] + [(yh ^ 1) * 4 + x]
    column += [(yh ^ 1) * 4 + (x + 2) % 4, yh * 4 + (x + 2) % 4]
    column += [(yh ^ 1) * 4 + (x + j) % 4 for j in (behind, ahead)]
    places = [[(c // 2 - z) % 4 for c in column], [c % 2 ^ yl for c in column], [c // 2 for c in column]]
    places = jnp.stack([jnp.stack(row) for row in places]).astype(jnp.int32)
    first = (out_weight, *first, far_opposite)
    other, early = lax.optimization_barrier((other, project_early(gated, first)))
    near = project(project_other_kernel, (2, 4), other, places, (*first, onward, across))
    near, gated = lax.optimization_barrier((near, gated))
    away = project(project_own_kernel, (4, 2), gated, places, (early, onward, across))
    pair = add_pair(near[0], shift(near[1], "yl", 1))
    got = shift(add_up(*lax.all_to_all(pair, "z", 0, 0)), "core", 1)
    ring = add_up(away[0], *[shift(away[j], "z", j) for j in (1, 3, 2)])
    kept = add_up(ring[0], shift(ring[1], "yl", 1))
    return jnp.where(
        core == 0, jnp.concatenate([kept, got], 1), jnp.concatenate([got, kept], 1)
    )


def solution(mesh):
    fine = Mesh(
        mesh.devices.reshape(tuple(SIZES[name] for name in ALL)),
        ALL,
    )
    return jax.shard_map(
        body,
        mesh=fine,
        in_specs=(
            P(SEQ, CH),
            P(SEQ, CH),
            P(SEQ, CH),
            P(CH, None),
            P(CH, None),
            P(CH),
            P(CH, SEQ),
        ),
        out_specs=P(SEQ, CH),
        check_vma=False,
    )
```
